1024 devices in a mesh: dp: 16 (over z, core), expert: 64 (over x, y).
Axes of the slice: x: 8, y: 8, z: 8, core: 2. Of those that a mesh axis runs over, the one named last changes fastest.
Arguments:
- grad_out: bfloat16 [131072, 1024], P(('dp', 'expert')), may hold values from -6 to 6
- routes: int32 [131072, 2], P(('dp', 'expert')), may hold values from 0 to 255, all different within a row; in each aligned block of 128 rows (0 to 127, 128 to 255, ...) at most 2 rows name the same one
- gates: float32 [131072, 2], P(('dp', 'expert')), may hold values from 0.2 to 1
- weights: bfloat16 [64, 3584, 1024], P('expert'), may hold values from -0.1875 to 0.1875
- saved_inputs: bfloat16 [16, 64, 128, 3584], P('dp', 'expert'), may hold values from -0.29882812 to 0.29882812
Outputs:
- input_grad: bfloat16 [131072, 3584], P(('dp', 'expert'))
- weight_grad: bfloat16 [64, 3584, 1024], P('expert', 'dp')
The draws below stay inside these ranges and needn't reach their ends.
Inputs may be any that keep to these rules, and one draw needn't show every extreme that they name: `routes`: each row names 2 different experts. Expert e < 64 is held on index e of expert. Among the tokens of one device no expert is named more than 2 times. Entries of saved_inputs whose slot is empty are never read.
All inputs are finite; a program needn't handle non-finite values.
Results may differ from the reference program's by a relative error of at most 0.025.
Values may be sent and summed in bfloat16 or wider, within the bound.
A program may use at most 64 MiB of HBM per device.

```python
import math
import jax
import jax.numpy as jnp
import numpy as np
from jax import lax

D = 3584
FF = 1024
TOP = 2
TOK_DEV = 128
EXPERTS = 64
ROUTED = 256
CAP = 2
TOKENS = 131072
N_DP = 16
N_EXPERT = 64


def strengthened(values, key, source, target, shards_of, factor):
    owner, partner = [(jnp.arange(values.shape[position]) // (values.shape[position] // shards_of)).reshape([-1 if axis == position else 1 for axis in range(values.ndim)]) for position in (source, target)]
    chosen = jax.random.permutation(key, shards_of)[partner]
    strong = (owner == chosen) | (owner == (partner + shards_of // 2) % shards_of)
    return jnp.where(strong, factor * values, values)


def shard_levels(key, dims, cuts, least, largest):
    def one(dim, blocks):
        steps = jax.random.uniform(jax.random.fold_in(jax.random.fold_in(key, 6), dim), (blocks,), jnp.float32, least / len(cuts), largest / len(cuts))
        return jnp.repeat(jnp.exp(steps), dims[dim] // blocks).reshape((-1,) + (1,) * (len(dims) - dim - 1))

    level = one(*cuts[0])
    for cut in cuts[1:]:
        level = level * one(*cut)
    return level


def routed_block(stream_key, own, number, rows, amount, top, most, lean):
    sequence = jax.random.permutation(stream_key, amount)
    crowded, usual = portions_of(amount, rows * top, most, lean, True), portions_of(amount, rows * top, most, lean, False)
    places = jnp.arange(amount)

    def named(sizes, turn):
        used = int((sizes > 0).sum())
        fixed = max(1, used // 4)
        shifted = fixed + (places - fixed + turn * (used - fixed)) % max(1, amount - fixed)
        return jnp.zeros((amount,), jnp.int32).at[sequence[jnp.where(places < fixed, places, shifted)]].set(jnp.asarray(sizes, jnp.int32))

    sizes = jnp.where(number % 4 == 0, named(crowded, number // 4), named(usual, number - number // 4 - 1))
    mixed = jax.random.permutation(jax.random.fold_in(own, 3), amount)
    giver, taker = mixed[0:amount // 2 * 2:2], mixed[1:amount // 2 * 2:2]
    room = jnp.minimum(sizes[giver] - 1, most - sizes[taker]) // 2
    room = jnp.where((giver == sequence[0]) | (taker == sequence[0]) | (sizes[taker] == 0), 0, jnp.maximum(room, 0))
    shifted = jax.random.randint(jax.random.fold_in(own, 4), (amount // 2,), 0, 1 << 20) % (room + 1)
    sizes = sizes.at[giver].add(-shifted).at[taker].add(shifted)
    members = jnp.searchsorted(jnp.cumsum(sizes), jnp.arange(rows * top), side="right").astype(jnp.int32)
    grid = members.reshape(top, rows).T
    grid = grid[jax.random.permutation(jax.random.fold_in(own, 1), rows)]
    turn = jax.random.randint(jax.random.fold_in(own, 2), (rows, 1), 0, top)
    return jnp.take_along_axis(grid, (jnp.arange(top)[None, :] + turn) % top, axis=1)


def portions_of(number_of, total, most, slope, full):
    weights = [(1 << 20) // math.isqrt(standing ** slope) + 1 for standing in range(1, number_of + 1)]
    largest = most if full else min(most, max(-(-total // number_of), total * weights[0] // sum(weights)))
    least = 1 if total - largest >= number_of - 1 else 0
    given, rest = [largest] + [least] * (number_of - 1), total - largest - least * (number_of - 1)
    while rest > 0:
        movable = [i for i in range(1, number_of) if given[i] < largest] or [i for i in range(1, number_of) if given[i] < most]
        whole, budget = sum([weights[i] for i in movable]), rest
        for i in movable:
            extra = min(most - given[i], max(1, budget * weights[i] // whole), rest)
            given[i] = given[i] + extra
            rest = rest - extra
    return np.array(given)


def noise(rng, extent, scale, reach, cuts=(), held_as=jnp.bfloat16):
    entries = jax.random.normal(rng, extent, jnp.float32) * scale
    if len(cuts) > 0:
        entries = shard_levels(rng, extent, cuts, -0.22, 0.18) * entries
    return jnp.clip(entries, min=-reach, max=reach).astype(held_as)


def noise_with(key, extent, deviation, limit, shards, heavy, held_as=jnp.bfloat16):
    values = deviation * jax.random.normal(key, extent, jnp.float32)
    if shards:
        values = values * shard_levels(key, extent, shards, -0.22, 0.18)
    return jnp.clip(strengthened(values, jax.random.fold_in(key, 3), *heavy), -limit, limit).astype(held_as)


def setup_inputs(seed: int = 0) -> dict:
    splits = jax.random.split(jax.random.key(seed), 6)
    grad_out = noise(splits[0], (TOKENS, FF), 1.0, 6.0, ((0, 1024),))
    routes_keys = jax.random.split(jax.random.fold_in(splits[1], 1), TOKENS // TOK_DEV)
    routes_turns = jax.random.permutation(jax.random.fold_in(splits[1], 3), TOKENS // TOK_DEV)
    routes = jax.vmap(lambda own, number: routed_block(jax.random.fold_in(splits[1], 2), own, number, TOK_DEV, ROUTED, TOP, CAP, 2))(routes_keys, routes_turns).reshape((TOKENS, TOP))
    gates = jnp.clip(0.2 + 0.8 * jax.random.uniform(splits[2], (TOKENS, TOP), jnp.float32) ** shard_levels(splits[2], (TOKENS, TOP), ((0, 1024),), -0.2, 0.2), 0.2, 1.0)
    weights = noise(splits[3], (EXPERTS, D, FF), FF ** -0.5, 0.1875, ((0, 64),))
    saved_inputs = noise_with(splits[4], (N_DP, EXPERTS, EXPERTS * CAP, D), 0.05, 0.29882812, ((0, 16), (1, 64)), (0, 3, 16, 2.0))
    return {"grad_out": grad_out, "routes": routes, "gates": gates, "weights": weights, "saved_inputs": saved_inputs}


def slot_tables(id_row):
    onehot = (id_row[:, None] == jnp.arange(EXPERTS, dtype=jnp.int32)[None, :]).astype(jnp.int32)
    ranking = jnp.cumsum(onehot, axis=0) - onehot
    placed = jnp.sum(ranking * onehot, axis=1)
    inside = jnp.sum(onehot, axis=1)
    target = jnp.where(inside > 0, id_row * CAP + placed, EXPERTS * CAP).astype(jnp.int32)
    return target, inside


def reference(grad_out, routes, gates, weights, saved_inputs):
    blocks = N_DP * N_EXPERT
    slot_count = TOK_DEV * TOP
    slots_all = EXPERTS * CAP
    grad_blocks = grad_out.reshape(blocks, TOK_DEV, FF)
    id_blocks = routes.reshape(blocks, slot_count)
    gate_blocks = gates.reshape(blocks, slot_count)
    targets, insides = jax.vmap(slot_tables)(id_blocks)
    token_of_slot = jnp.arange(slot_count, dtype=jnp.int32) // TOP

    def build(grad_block, target, gate_row, inside):
        rows_out = jnp.zeros((slots_all + 1, FF), jnp.bfloat16).at[target].set(grad_block[token_of_slot])
        gate_out = jnp.zeros((slots_all + 1,), jnp.float32).at[target].set(jnp.where(inside > 0, gate_row, 0.0))
        return rows_out[:slots_all], gate_out[:slots_all]

    sent_rows, sent_gates = jax.vmap(build)(grad_blocks, targets, gate_blocks, insides)
    sent_rows = sent_rows.reshape(N_DP, N_EXPERT, EXPERTS, CAP, FF)
    sent_gates = sent_gates.reshape(N_DP, N_EXPERT, EXPERTS, CAP)
    recv_rows = jnp.transpose(sent_rows, (2, 0, 1, 3, 4)).reshape(EXPERTS, N_DP, N_EXPERT * CAP, FF)
    recv_gates = jnp.transpose(sent_gates, (2, 0, 1, 3)).reshape(EXPERTS, N_DP, N_EXPERT * CAP)
    saved_by_expert = jnp.transpose(saved_inputs, (1, 0, 2, 3))

    def expert_work(operands):
        rows_e, gates_e, weight_e, saved_e = operands
        answers = jnp.einsum("prf,df->prd", rows_e.astype(jnp.float32), weight_e.astype(jnp.float32)).astype(jnp.bfloat16)
        scaled = (gates_e[:, :, None] * rows_e.astype(jnp.float32)).astype(jnp.bfloat16)
        partials = jnp.einsum("prd,prf->pdf", saved_e.astype(jnp.float32), scaled.astype(jnp.float32))
        rounded = lax.optimization_barrier(partials.astype(jnp.bfloat16)).astype(jnp.float32)
        return answers, jnp.sum(rounded, axis=0).astype(jnp.bfloat16)

    answers_all, weight_grad = lax.map(expert_work, (recv_rows, recv_gates, weights, saved_by_expert))
    flat_answers = answers_all.reshape(-1, D)

    def combine(operands):
        block_id, target, gate_row, inside = operands
        replica = block_id // N_EXPERT
        source = block_id % N_EXPERT
        expert_id = target // CAP
        slot_pos = target % CAP
        row_index = ((expert_id * N_DP + replica) * N_EXPERT + source) * CAP + slot_pos
        row_index = jnp.where(inside > 0, row_index, 0).astype(jnp.int32)
        picked = flat_answers[row_index]
        weight_slot = jnp.where(inside > 0, gate_row, 0.0)
        summed = jnp.sum(picked.reshape(TOK_DEV, TOP, D).astype(jnp.float32) * weight_slot.reshape(TOK_DEV, TOP, 1), axis=1)
        return summed.astype(jnp.bfloat16)

    input_grad = lax.map(combine, (jnp.arange(blocks, dtype=jnp.int32), targets, gate_blocks, insides))
    return input_grad.reshape(TOKENS, D), weight_grad
```

```python
import jax
import jax.numpy as jnp
from jax import lax
from jax.sharding import PartitionSpec as P


def on_device(grad_out, routes, gates, weights, saved_inputs):
    experts = lax.axis_size("expert")
    tok_rows, ff = grad_out.shape
    slots_all = saved_inputs.shape[2]
    capacity = slots_all // experts
    model_width = saved_inputs.shape[3]
    saved_rows = saved_inputs.reshape(slots_all, model_width)
    saved_band = lax.all_to_all(saved_rows, "dp", split_axis=1, concat_axis=0, tiled=True)

    ids, gate_rows = routes.T, gates.T
    slot = lax.broadcasted_iota(jnp.int32, (slots_all, tok_rows), 0)
    slot_expert, slot_rank = slot // capacity, slot % capacity
    hits = [slot_expert == ids[k][None, :] for k in range(ids.shape[0])]
    named = (hits[0] | hits[1]).astype(jnp.bfloat16)
    row = lax.broadcasted_iota(jnp.int32, (tok_rows, tok_rows), 0)
    column = lax.broadcasted_iota(jnp.int32, (tok_rows, tok_rows), 1)
    earlier = jnp.dot(named, (row < column).astype(jnp.bfloat16), preferred_element_type=jnp.float32)
    filled = (hits[0] | hits[1]) & (earlier == slot_rank.astype(jnp.float32))
    gate = jnp.where(hits[0], gate_rows[0][None, :], gate_rows[1][None, :])
    slot_gate = jnp.sum(jnp.where(filled, gate, 0.0), axis=1, keepdims=True)
    table = filled.astype(jnp.bfloat16)

    picked = jnp.dot(table, grad_out, preferred_element_type=jnp.float32)
    scaled_out = (picked * slot_gate).astype(jnp.bfloat16)
    scaled = lax.all_to_all(
        scaled_out.reshape(experts, capacity, ff), "expert", split_axis=0, concat_axis=0, tiled=True
    ).reshape(slots_all, ff)

    scaled_all = lax.all_gather(scaled, "dp", axis=0, tiled=True)
    answers = lax.dot_general(
        scaled, weights[0], (((1,), (1,)), ((), ())), preferred_element_type=jnp.float32
    ).astype(jnp.bfloat16)
    returned = lax.all_to_all(
        answers.reshape(experts, capacity, model_width), "expert", split_axis=0, concat_axis=0, tiled=True
    ).reshape(slots_all, model_width)
    input_grad = lax.dot_general(
        table, returned, (((0,), (0,)), ((), ())), preferred_element_type=jnp.float32
    ).astype(jnp.bfloat16)
    weight_grad = lax.dot_general(
        saved_band, scaled_all, (((0,), (0,)), ((), ())), preferred_element_type=jnp.float32
    ).astype(jnp.bfloat16)
    return input_grad, weight_grad[None]


def solution(mesh):
    return jax.shard_map(
        on_device,
        mesh=mesh,
        in_specs=(
            P(("dp", "expert"), None),
            P(("dp", "expert"), None),
            P(("dp", "expert"), None),
            P("expert", None, None),
            P("dp", "expert", None, None),
        ),
        out_specs=(P(("dp", "expert"), None), P("expert", "dp", None)),
        check_vma=False,
    )
```

```python
import functools

import jax
import jax.numpy as jnp
from jax import lax
from jax.experimental import pallas as pl
from jax.experimental.pallas import tpu as pltpu
from jax.sharding import PartitionSpec as P

MESH = pl.DeviceIdType.MESH
BF16, F32 = jnp.bfloat16, jnp.float32


def nn(a, b):
    return jnp.dot(a, b, preferred_element_type=F32)


def nt(a, b):
    return lax.dot_general(a, b, (((1,), (1,)), ((), ())), preferred_element_type=F32)


def kernel(
    side, chips,
    ids_hbm, gates_hbm, grad_hbm, w_hbm, saved_hbm,
    input_grad, weight_grad,
    ids, gates, grad, w, saved, local_sems,
    rows_out1, rows_in1, rows_out2, rows_in2, rows_sems,
    saved_t, bands, band_sems,
    scaled_all, ring_send, ring_recv, sib_send, sib_recv,
    back_out1, back_in1, back_out2, back_in2, back_sems,
    total,
):
    slots, width = saved.shape
    ff = grad.shape[1]
    half = ff // 2
    part = width // 4
    block = slots // side
    band = bands.shape[1]
    bits = side.bit_length() - 1
    rounds = chips // 2
    rep, spot = lax.axis_index("dp"), lax.axis_index("expert")
    mz, core = lax.div(rep, 2), lax.rem(rep, 2)
    mx, my = lax.div(spot, side), lax.rem(spot, side)

    def along_x(k):
        return {"expert": lax.rem(mx + k, side) * side + my}

    def along_y(k):
        return {"expert": mx * side + lax.rem(my + k, side)}

    def chip_at(k):
        return lax.rem(mz + k + chips, chips)

    barrier = pltpu.get_barrier_semaphore()
    for k in range(1, side):
        pl.semaphore_signal(barrier, inc=1, device_id=along_x(k), device_id_type=MESH)
        pl.semaphore_signal(barrier, inc=1, device_id=along_y(k), device_id_type=MESH)
    for k in range(1, 2 * chips):
        pl.semaphore_signal(
            barrier, inc=1, device_id={"dp": lax.rem(rep + k, 2 * chips)}, device_id_type=MESH
        )

    loads = [
        pltpu.make_async_copy(source, target, local_sems.at[i])
        for i, (source, target) in enumerate(
            ((ids_hbm, ids), (gates_hbm, gates), (grad_hbm, grad), (saved_hbm, saved), (w_hbm, w))
        )
    ]
    for load in loads:
        load.start()

    row = lax.broadcasted_iota(jnp.int32, (slots, slots), 0)
    column = lax.broadcasted_iota(jnp.int32, (slots, slots), 1)
    pair = row >> 1
    swapped = ((pair & (side - 1)) << bits) | (pair >> bits)
    swap = (column == ((swapped << 1) | (row & 1))).astype(F32).astype(BF16)
    same = (row == column).astype(F32).astype(BF16)

    tokens = grad.shape[0]
    slot = lax.broadcasted_iota(jnp.int32, (slots, tokens), 0)
    token_row = lax.broadcasted_iota(jnp.int32, (tokens, tokens), 0)
    token_column = lax.broadcasted_iota(jnp.int32, (tokens, tokens), 1)
    before = (token_row < token_column).astype(F32).astype(BF16)
    eye = (token_row == token_column).astype(F32).astype(BF16)
    for load in loads[:2]:
        load.wait()

    def table_of(expert):
        first, second = expert == ids[0:1, :], expert == ids[1:2, :]
        named = (first | second).astype(F32)
        earlier = nn(named.astype(BF16), before)
        rank = (slot & 1).astype(F32)
        table = jnp.where(earlier == rank, named, 0.0)
        gate = jnp.where(first, gates[0:1, :], jnp.where(second, gates[1:2, :], 0.0))
        slot_gate = jnp.sum(table * gate, axis=1, keepdims=True)
        return table.astype(BF16), slot_gate

    expert = slot >> 1
    table_xy, gate_xy = table_of(expert)
    table_yx, gate_yx = table_of(((expert & (side - 1)) << bits) | (expert >> bits))
    loads[2].wait()
    rows_out1[0] = (nn(table_xy, grad[:, :half]) * gate_xy).astype(BF16)
    rows_out1[1] = (nn(table_yx, grad[:, half:]) * gate_yx).astype(BF16)

    pl.semaphore_wait(barrier, 2 * (side - 1) + 2 * chips - 1)

    def spread(out, into, sems, to_x):
        me, where = (mx, along_x) if to_x else (my, along_y)
        for k in range(1, side):
            there = lax.rem(me + k, side)
            pltpu.make_async_remote_copy(
                src_ref=out.at[pl.ds(pl.multiple_of(there * block, block), block), :],
                dst_ref=into.at[pl.ds(pl.multiple_of(me * block, block), block), :],
                send_sem=sems.at[0],
                recv_sem=sems.at[1],
                device_id=where(k),
                device_id_type=MESH,
            ).start()
        own = pl.ds(pl.multiple_of(me * block, block), block)
        into[own, :] = out[own, :]

    def spread_wait(out, into, sems):
        rest = pl.ds(0, slots - block)
        return pltpu.make_async_remote_copy(
            src_ref=out.at[rest, :],
            dst_ref=into.at[rest, :],
            send_sem=sems.at[0],
            recv_sem=sems.at[1],
            device_id=along_x(1),
            device_id_type=MESH,
        )

    def rows(hop, i):
        out, into = ((rows_out1, rows_in1), (rows_out2, rows_in2))[hop]
        return out.at[i], into.at[i], rows_sems.at[2 * hop + i]

    for i in range(2):
        spread(*rows(0, i), to_x=i == 0)

    loads[3].wait()
    for start in range(0, width, slots):
        saved_t[pl.ds(start, slots), :] = nt(same, saved[:, start : start + slots]).astype(BF16)

    def send_bands(first, last):
        for k in range(first, last):
            for other in range(2):
                if k == 0 and other == 0:
                    continue
                there = chip_at(k) * 2 + lax.rem(core + other, 2)
                pltpu.make_async_remote_copy(
                    src_ref=saved_t.at[pl.ds(pl.multiple_of(there * band, band), band), :],
                    dst_ref=bands.at[mz, :, pl.ds(pl.multiple_of(core * slots, slots), slots)],
                    send_sem=band_sems.at[0, other if k else 2],
                    recv_sem=band_sems.at[1, other if k else 2],
                    device_id={"dp": there},
                    device_id_type=MESH,
                ).start()

    def band_wait(j):
        count = 1 if j == 2 else chips - 1
        some = bands.at[pl.ds(0, count), :, pl.ds(0, slots)]
        return pltpu.make_async_remote_copy(
            src_ref=some,
            dst_ref=some,
            send_sem=band_sems.at[0, j],
            recv_sem=band_sems.at[1, j],
            device_id={"dp": lax.rem(rep + 1, 2 * chips)},
            device_id_type=MESH,
        )

    EARLY(send_bands, chips, 0)
    bands[mz, :, pl.ds(pl.multiple_of(core * slots, slots), slots)] = saved_t[
        pl.ds(pl.multiple_of(rep * band, band), band), :
    ]

    for i in range(2):
        spread_wait(*rows(0, i)).wait_recv()
        rows_out2[i] = nn(swap, rows_in1[i]).astype(BF16)
        spread(*rows(1, i), to_x=i == 1)
    EARLY(send_bands, chips, 1)
    own_rows = pl.ds(pl.multiple_of(rep * slots, slots), slots)
    for i in range(2):
        spread_wait(*rows(1, i)).wait_recv()
    scaled_all[own_rows, pl.ds(0, half)] = nn(swap, rows_in2[0]).astype(BF16)
    scaled_all[own_rows, pl.ds(half, half)] = rows_in2[1]

    def piece(chip, which, h):
        return scaled_all.at[
            pl.ds(pl.multiple_of((chip * 2 + which) * slots, slots), slots), pl.ds(h * half, half)
        ]

    def hops(r):
        return [(0, 0), (1, 0), (0, 1), (1, 1)] if r < rounds else [(0, 0), (1, 1)]

    def ring(r, way, h):
        sign = 1 if way == 0 else -1
        ref = piece(chip_at(-sign * (r - 1)), core, h)
        return pltpu.make_async_remote_copy(
            src_ref=ref,
            dst_ref=ref,
            send_sem=ring_send.at[r - 1, way, h],
            recv_sem=ring_recv.at[r - 1, way, h],
            device_id={"dp": chip_at(sign) * 2 + core},
            device_id_type=MESH,
        )

    def sibling(r, way, h):
        sign = 1 if way == 0 else -1
        ref = piece(chip_at(-sign * r), core, h)
        return pltpu.make_async_remote_copy(
            src_ref=ref,
            dst_ref=ref,
            send_sem=sib_send.at[r, way, h],
            recv_sem=sib_recv.at[r, way, h],
            device_id={"dp": mz * 2 + 1 - core},
            device_id_type=MESH,
        )

    def ring_step(r):
        for way, h in hops(r):
            ring(r, way, h).wait_recv()
            if r < rounds and (way, h) in hops(r + 1):
                ring(r + 1, way, h).start()
            sibling(r, way, h).start()

    for way, h in hops(1):
        ring(1, way, h).start()
    for h in range(2):
        sibling(0, 0, h).start()
    EARLY(send_bands, chips, 2)

    scaled_xy = scaled_all[own_rows, :]
    scaled_yx = nn(swap, scaled_xy).astype(BF16)
    loads[4].wait()

    def back(hop, q):
        out, into = ((back_out1, back_in1), (back_out2, back_in2))[hop]
        return out.at[q], into.at[q], back_sems.at[4 * hop + q]

    for q in (0, 2, 1, 3):
        lhs = scaled_xy if q < 2 else scaled_yx
        back_out1[q] = nt(lhs, w[pl.ds(q * part, part), :]).astype(BF16)
        spread(*back(0, q), to_x=q < 2)

    def turn(q):
        spread_wait(*back(0, q)).wait_recv()
        back_out2[q] = nn(swap, back_in1[q]).astype(BF16)
        spread(*back(1, q), to_x=q >= 2)

    table_back = [nt(eye, table).astype(BF16) for table in (table_yx, table_xy)]

    def combine(q):
        spread_wait(*back(1, q)).wait_recv()
        input_grad[:, pl.ds(q * part, part)] = nn(table_back[q // 2], back_in2[q]).astype(BF16)

    def product(chip):
        at = pl.ds(pl.multiple_of(chip * 2 * slots, 2 * slots), 2 * slots)
        return nn(bands[chip], scaled_all[at, :])

    jobs = [[(turn, 0), (turn, 2)], [(turn, 1), (turn, 3)], [(combine, 0), (combine, 2)], [(combine, 1), (combine, 3)]]
    for r in range(1, max(rounds, 4) + 1):
        if r <= 4:
            for job, q in jobs[r - 1]:
                job(q)
        if r < rounds:
            ring_step(r)

    for j in range(3):
        band_wait(j).wait_recv()
    for h in range(2):
        sibling(0, 0, h).wait_recv()
    total[...] = product(mz)
    for r in range(1, rounds):
        for way, h in hops(r):
            sibling(r, way, h).wait_recv()
        total[...] += product(chip_at(-r))
        total[...] += product(chip_at(r))
    ring_step(rounds)
    for way, h in hops(rounds):
        sibling(rounds, way, h).wait_recv()
    weight_grad[...] = (total[...] + product(chip_at(rounds))).astype(BF16)

    for i in range(2):
        for hop in range(2):
            spread_wait(*rows(hop, i)).wait_send()
    for q in range(4):
        for hop in range(2):
            spread_wait(*back(hop, q)).wait_send()
    for j in range(3):
        band_wait(j).wait_send()
    for h in range(2):
        sibling(0, 0, h).wait_send()
    for r in range(1, rounds + 1):
        for way, h in hops(r):
            ring(r, way, h).wait_send()
            sibling(r, way, h).wait_send()


def EARLY(send_bands, chips, place):
    if place == 0:
        send_bands(0, chips)


def on_device(side, grad_out, routes, gates, weights, saved_inputs):
    replicas = lax.axis_size("dp")
    chips = replicas // 2
    slots, width = saved_inputs.shape[2:]
    tokens, ff = grad_out.shape
    half, part, band = ff // 2, width // 4, width // replicas
    rounds = chips // 2
    ids, gate_rows = routes.T, gates.T
    dma = pltpu.SemaphoreType.DMA
    scratch = [
        pltpu.VMEM(ids.shape, jnp.int32),
        pltpu.VMEM(gate_rows.shape, F32),
        pltpu.VMEM((tokens, ff), BF16),
        pltpu.VMEM((width, ff), BF16),
        pltpu.VMEM((slots, width), BF16),
        dma((5,)),
        *[pltpu.VMEM((2, slots, half), BF16)] * 4,
        dma((4, 2)),
        pltpu.VMEM((width, slots), BF16),
        pltpu.VMEM((chips, band, 2 * slots), BF16),
        dma((2, 3)),
        pltpu.VMEM((replicas * slots, ff), BF16),
        dma((rounds, 2, 2)),
        dma((rounds, 2, 2)),
        dma((rounds + 1, 2, 2)),
        dma((rounds + 1, 2, 2)),
        *[pltpu.VMEM((4, slots, part), BF16)] * 4,
        dma((8, 2)),
        pltpu.VMEM((band, ff), F32),
    ]
    input_grad, weight_grad = pl.pallas_call(
        functools.partial(kernel, side, chips),
        out_shape=(
            jax.ShapeDtypeStruct((tokens, width), BF16),
            jax.ShapeDtypeStruct((band, ff), BF16),
        ),
        in_specs=[pl.BlockSpec(memory_space=pl.ANY)] * 5,
        out_specs=[pl.BlockSpec(memory_space=pltpu.VMEM)] * 2,
        scratch_shapes=scratch,
        compiler_params=pltpu.CompilerParams(
            collective_id=0, has_side_effects=True, vmem_limit_bytes=48 << 20
        ),
    )(ids, gate_rows, grad_out, weights.reshape(width, ff), saved_inputs.reshape(slots, width))
    return input_grad, weight_grad[None]


def solution(mesh):
    side = int(round(mesh.shape["expert"] ** 0.5))
    return jax.shard_map(
        functools.partial(on_device, side),
        mesh=mesh,
        in_specs=(
            P(("dp", "expert"), None),
            P(("dp", "expert"), None),
            P(("dp", "expert"), None),
            P("expert", None, None),
            P("dp", "expert", None, None),
        ),
        out_specs=(P(("dp", "expert"), None), P("expert", "dp", None)),
        check_vma=False,
    )
```

```python
import functools

import jax
import jax.numpy as jnp
from jax import lax
from jax.experimental import pallas as pl
from jax.experimental.pallas import tpu as pltpu
from jax.sharding import PartitionSpec as P

MESH = pl.DeviceIdType.MESH
PIECES = 2
BF16, F32 = jnp.bfloat16, jnp.float32


def nn(a, b):
    return jnp.dot(a, b, preferred_element_type=F32)


def nt(a, b):
    return lax.dot_general(a, b, (((1,), (1,)), ((), ())), preferred_element_type=F32)


def kernel(
    side, chips,
    ids_hbm, gates_hbm, grad_hbm, w_hbm, saved_hbm,
    input_grad_hbm, weight_grad_hbm,
    ids, gates, grad, w, saved, local_sems,
    rows_out1, rows_in1, rows_out2, rows_in2, rows_sems,
    saved_t, bands, band_sems,
    scaled_all, ring_send, ring_recv, sib_send, sib_recv,
    back_out1, back_in1, back_out2, back_in2, back_sems,
    total, input_grad, weight_grad, store_sems,
):
    slots, width = saved.shape
    ff = grad.shape[1]
    half = ff // 2
    part = width // 4
    block = slots // side
    band = bands.shape[1]
    bits = side.bit_length() - 1
    rounds = chips // 2
    cut = ff // PIECES
    rep, spot = lax.axis_index("dp"), lax.axis_index("expert")
    mz, core = lax.div(rep, 2), lax.rem(rep, 2)
    mx, my = lax.div(spot, side), lax.rem(spot, side)

    def along_x(k):
        return {"expert": lax.rem(mx + k, side) * side + my}

    def along_y(k):
        return {"expert": mx * side + lax.rem(my + k, side)}

    def chip_at(k):
        return lax.rem(mz + k + chips, chips)

    barrier = pltpu.get_barrier_semaphore()
    for k in range(1, side):
        pl.semaphore_signal(barrier, inc=1, device_id=along_x(k), device_id_type=MESH)
        pl.semaphore_signal(barrier, inc=1, device_id=along_y(k), device_id_type=MESH)
    for k in range(1, 2 * chips):
        pl.semaphore_signal(
            barrier, inc=1, device_id={"dp": lax.rem(rep + k, 2 * chips)}, device_id_type=MESH
        )

    loads = [
        pltpu.make_async_copy(source, target, local_sems.at[i])
        for i, (source, target) in enumerate(
            ((ids_hbm, ids), (gates_hbm, gates), (grad_hbm, grad), (saved_hbm, saved), (w_hbm, w))
        )
    ]
    for load in loads:
        load.start()

    row = lax.broadcasted_iota(jnp.int32, (slots, slots), 0)
    column = lax.broadcasted_iota(jnp.int32, (slots, slots), 1)
    pair = row >> 1
    swapped = ((pair & (side - 1)) << bits) | (pair >> bits)
    swap = (column == ((swapped << 1) | (row & 1))).astype(F32).astype(BF16)
    same = (row == column).astype(F32).astype(BF16)

    tokens = grad.shape[0]
    slot = lax.broadcasted_iota(jnp.int32, (slots, tokens), 0)
    token_row = lax.broadcasted_iota(jnp.int32, (tokens, tokens), 0)
    token_column = lax.broadcasted_iota(jnp.int32, (tokens, tokens), 1)
    before = (token_row < token_column).astype(F32).astype(BF16)
    eye = (token_row == token_column).astype(F32).astype(BF16)
    for load in loads[:2]:
        load.wait()

    def table_of(expert):
        first, second = expert == ids[0:1, :], expert == ids[1:2, :]
        named = (first | second).astype(F32)
        earlier = nn(named.astype(BF16), before)
        rank = (slot & 1).astype(F32)
        table = jnp.where(earlier == rank, named, 0.0)
        gate = jnp.where(first, gates[0:1, :], jnp.where(second, gates[1:2, :], 0.0))
        slot_gate = jnp.sum(table * gate, axis=1, keepdims=True)
        return table.astype(BF16), slot_gate

    expert = slot >> 1
    table_xy, gate_xy = table_of(expert)
    table_yx, gate_yx = table_of(((expert & (side - 1)) << bits) | (expert >> bits))
    loads[2].wait()
    rows_out1[0] = (nn(table_xy, grad[:, :half]) * gate_xy).astype(BF16)
    rows_out1[1] = (nn(table_yx, grad[:, half:]) * gate_yx).astype(BF16)

    loads[3].wait()
    for start in range(0, width, slots):
        saved_t[pl.ds(start, slots), :] = nt(same, saved[:, start : start + slots]).astype(BF16)

    pl.semaphore_wait(barrier, 2 * (side - 1) + 2 * chips - 1)

    def spread(out, into, sems, to_x):
        me, where = (mx, along_x) if to_x else (my, along_y)
        for k in range(1, side):
            there = lax.rem(me + k, side)
            pltpu.make_async_remote_copy(
                src_ref=out.at[pl.ds(pl.multiple_of(there * block, block), block), :],
                dst_ref=into.at[pl.ds(pl.multiple_of(me * block, block), block), :],
                send_sem=sems.at[0],
                recv_sem=sems.at[1],
                device_id=where(k),
                device_id_type=MESH,
            ).start()
        own = pl.ds(pl.multiple_of(me * block, block), block)
        into[own, :] = out[own, :]

    def spread_wait(out, into, sems):
        rest = pl.ds(0, slots - block)
        return pltpu.make_async_remote_copy(
            src_ref=out.at[rest, :],
            dst_ref=into.at[rest, :],
            send_sem=sems.at[0],
            recv_sem=sems.at[1],
            device_id=along_x(1),
            device_id_type=MESH,
        )

    def rows(hop, i):
        out, into = ((rows_out1, rows_in1), (rows_out2, rows_in2))[hop]
        return out.at[i], into.at[i], rows_sems.at[2 * hop + i]

    for i in range(2):
        spread(*rows(0, i), to_x=i == 0)

    def send_bands(first, last):
        for k in range(first, last):
            for other in range(2):
                if k == 0 and other == 0:
                    continue
                there = chip_at(k) * 2 + lax.rem(core + other, 2)
                pltpu.make_async_remote_copy(
                    src_ref=saved_t.at[pl.ds(pl.multiple_of(there * band, band), band), :],
                    dst_ref=bands.at[mz, :, pl.ds(pl.multiple_of(core * slots, slots), slots)],
                    send_sem=band_sems.at[0, other if k else 2],
                    recv_sem=band_sems.at[1, other if k else 2],
                    device_id={"dp": there},
                    device_id_type=MESH,
                ).start()

    def band_wait(j):
        count = 1 if j == 2 else chips - 1
        some = bands.at[pl.ds(0, count), :, pl.ds(0, slots)]
        return pltpu.make_async_remote_copy(
            src_ref=some,
            dst_ref=some,
            send_sem=band_sems.at[0, j],
            recv_sem=band_sems.at[1, j],
            device_id={"dp": lax.rem(rep + 1, 2 * chips)},
            device_id_type=MESH,
        )

    send_bands(0, chips)
    bands[mz, :, pl.ds(pl.multiple_of(core * slots, slots), slots)] = saved_t[
        pl.ds(pl.multiple_of(rep * band, band), band), :
    ]

    for i in range(2):
        spread_wait(*rows(0, i)).wait_recv()
        rows_out2[i] = nn(swap, rows_in1[i]).astype(BF16)
        spread(*rows(1, i), to_x=i == 1)
    own_rows = pl.ds(pl.multiple_of(rep * slots, slots), slots)
    for i in range(2):
        spread_wait(*rows(1, i)).wait_recv()
    scaled_all[own_rows, pl.ds(0, half)] = nn(swap, rows_in2[0]).astype(BF16)
    scaled_all[own_rows, pl.ds(half, half)] = rows_in2[1]

    def piece(chip, which, h):
        return scaled_all.at[
            pl.ds(pl.multiple_of((chip * 2 + which) * slots, slots), slots), pl.ds(h * cut, cut)
        ]

    def hops(r):
        if r < rounds:
            return [(way, h if way == 0 else PIECES - 1 - h) for h in range(PIECES) for way in range(2)]
        return [(way, h if way == 0 else PIECES - 1 - h) for h in range(PIECES // 2) for way in range(2)]

    def ring(r, way, h):
        sign = 1 if way == 0 else -1
        ref = piece(chip_at(-sign * (r - 1)), core, h)
        return pltpu.make_async_remote_copy(
            src_ref=ref,
            dst_ref=ref,
            send_sem=ring_send.at[r - 1, way, h],
            recv_sem=ring_recv.at[r - 1, way, h],
            device_id={"dp": chip_at(sign) * 2 + core},
            device_id_type=MESH,
        )

    def sibling(r, way, h):
        sign = 1 if way == 0 else -1
        ref = piece(chip_at(-sign * r), core, h)
        return pltpu.make_async_remote_copy(
            src_ref=ref,
            dst_ref=ref,
            send_sem=sib_send.at[r, way, h],
            recv_sem=sib_recv.at[r, way, h],
            device_id={"dp": mz * 2 + 1 - core},
            device_id_type=MESH,
        )

    def ring_step(r):
        for way, h in hops(r):
            ring(r, way, h).wait_recv()
            if r < rounds and (way, h) in hops(r + 1):
                ring(r + 1, way, h).start()
            sibling(r, way, h).start()

    for way, h in hops(1):
        ring(1, way, h).start()
    for h in range(PIECES):
        sibling(0, 0, h).start()

    scaled_xy = scaled_all[own_rows, :]
    scaled_yx = nn(swap, scaled_xy).astype(BF16)
    loads[4].wait()

    def back(hop, q):
        out, into = ((back_out1, back_in1), (back_out2, back_in2))[hop]
        return out.at[q], into.at[q], back_sems.at[4 * hop + q]

    for q in (0, 2, 1, 3):
        lhs = scaled_xy if q < 2 else scaled_yx
        back_out1[q] = nt(lhs, w[pl.ds(q * part, part), :]).astype(BF16)
        spread(*back(0, q), to_x=q < 2)

    def turn(q):
        spread_wait(*back(0, q)).wait_recv()
        back_out2[q] = nn(swap, back_in1[q]).astype(BF16)
        spread(*back(1, q), to_x=q >= 2)

    table_back = [nt(eye, table).astype(BF16) for table in (table_yx, table_xy)]

    def store_part(q):
        columns = pl.ds(q * part, part)
        return pltpu.make_async_copy(
            input_grad.at[:, columns], input_grad_hbm.at[:, columns], store_sems.at[q]
        )

    def combine(q):
        spread_wait(*back(1, q)).wait_recv()
        input_grad[:, pl.ds(q * part, part)] = nn(table_back[q // 2], back_in2[q]).astype(BF16)
        store_part(q).start()

    def product(chip):
        at = pl.ds(pl.multiple_of(chip * 2 * slots, 2 * slots), 2 * slots)
        return nn(bands[chip], scaled_all[at, :])

    def add(r):
        for way, h in hops(r):
            sibling(r, way, h).wait_recv()
        total[...] += product(chip_at(-r))
        total[...] += product(chip_at(r))

    jobs = [(turn, (0, 2)), (turn, (1, 3)), (combine, (0, 2)), (combine, (1, 3))]
    for r in range(1, max(rounds, 4) + 1):
        if r <= 4:
            job, parts = jobs[r - 1]
            for q in parts:
                job(q)
        if r < rounds:
            ring_step(r)

    for j in range(3):
        band_wait(j).wait_recv()
    for h in range(PIECES):
        sibling(0, 0, h).wait_recv()
    total[...] = product(mz)
    for r in range(1, rounds - 1):
        add(r)
    ring_step(rounds)
    if rounds > 1:
        add(rounds - 1)
    for way, h in hops(rounds):
        sibling(rounds, way, h).wait_recv()
    weight_grad[...] = (total[...] + product(chip_at(rounds))).astype(BF16)
    store = pltpu.make_async_copy(weight_grad, weight_grad_hbm, store_sems.at[4])
    store.start()

    for i in range(2):
        for hop in range(2):
            spread_wait(*rows(hop, i)).wait_send()
    for q in range(4):
        for hop in range(2):
            spread_wait(*back(hop, q)).wait_send()
    for j in range(3):
        band_wait(j).wait_send()
    for q in range(4):
        store_part(q).wait()
    for h in range(PIECES):
        sibling(0, 0, h).wait_send()
    for r in range(1, rounds + 1):
        for way, h in hops(r):
            ring(r, way, h).wait_send()
            sibling(r, way, h).wait_send()
    store.wait()


def on_device(side, grad_out, routes, gates, weights, saved_inputs):
    replicas = lax.axis_size("dp")
    chips = replicas // 2
    slots, width = saved_inputs.shape[2:]
    tokens, ff = grad_out.shape
    half, part, band = ff // 2, width // 4, width // replicas
    rounds = chips // 2
    ids, gate_rows = routes.T, gates.T
    dma = pltpu.SemaphoreType.DMA
    scratch = [
        pltpu.VMEM(ids.shape, jnp.int32),
        pltpu.VMEM(gate_rows.shape, F32),
        pltpu.VMEM((tokens, ff), BF16),
        pltpu.VMEM((width, ff), BF16),
        pltpu.VMEM((slots, width), BF16),
        dma((5,)),
        *[pltpu.VMEM((2, slots, half), BF16)] * 4,
        dma((4, 2)),
        pltpu.VMEM((width, slots), BF16),
        pltpu.VMEM((chips, band, 2 * slots), BF16),
        dma((2, 3)),
        pltpu.VMEM((replicas * slots, ff), BF16),
        dma((rounds, 2, PIECES)),
        dma((rounds, 2, PIECES)),
        dma((rounds + 1, 2, PIECES)),
        dma((rounds + 1, 2, PIECES)),
        *[pltpu.VMEM((4, slots, part), BF16)] * 4,
        dma((8, 2)),
        pltpu.VMEM((band, ff), F32),
        pltpu.VMEM((tokens, width), BF16),
        pltpu.VMEM((band, ff), BF16),
        dma((5,)),
    ]
    input_grad, weight_grad = pl.pallas_call(
        functools.partial(kernel, side, chips),
        out_shape=(
            jax.ShapeDtypeStruct((tokens, width), BF16),
            jax.ShapeDtypeStruct((band, ff), BF16),
        ),
        in_specs=[pl.BlockSpec(memory_space=pltpu.HBM)] * 5,
        out_specs=[pl.BlockSpec(memory_space=pltpu.HBM)] * 2,
        scratch_shapes=scratch,
        compiler_params=pltpu.CompilerParams(
            collective_id=0, has_side_effects=True, vmem_limit_bytes=61_000_000
        ),
    )(ids, gate_rows, grad_out, weights.reshape(width, ff), saved_inputs.reshape(slots, width))
    return input_grad, weight_grad[None]


def solution(mesh):
    side = int(round(mesh.shape["expert"] ** 0.5))
    return jax.shard_map(
        functools.partial(on_device, side),
        mesh=mesh,
        in_specs=(
            P(("dp", "expert"), None),
            P(("dp", "expert"), None),
            P(("dp", "expert"), None),
            P("expert", None, None),
            P("dp", "expert", None, None),
        ),
        out_specs=(P(("dp", "expert"), None), P("expert", "dp", None)),
        check_vma=False,
    )
```
